128 devices in a mesh: row: 16 (over z, y), col: 8 (over x, core).
Axes of the slice: x: 4, y: 4, z: 4, core: 2. Of those that a mesh axis runs over, the one named last changes fastest.
Arguments:
- frames: bfloat16 [16384, 4096], P('row', 'col'), may hold values from -6 to 6
- w_value: bfloat16 [4096, 4096], P('row', 'col'), may hold values from -0.09375 to 0.09375
- w_gate: bfloat16 [4096, 4096], P('row', 'col'), may hold values from -0.09375 to 0.09375
- taps: bfloat16 [31, 4096], P(None, 'col'), may hold values from -1 to 1
- grad_out: bfloat16 [16384, 4096], P('row', 'col'), may hold values from -4 to 4
Outputs:
- activated: bfloat16 [16384, 4096], P('row', 'col')
- grad_frames: bfloat16 [16384, 4096], P('row', 'col')
- grad_value: bfloat16 [4096, 4096], P('row', 'col')
- grad_gate: bfloat16 [4096, 4096], P('row', 'col')
- grad_taps: float32 [31, 4096], P(None, 'col')
The draws below stay inside these ranges and needn't reach their ends.
All inputs are finite; a program needn't handle non-finite values.
Results may differ from the reference program's by a relative error of at most 0.019.
Values may be sent and summed in bfloat16 or wider, within the bound.
No kernel may reach another device: no remote copies, remote signals or barrier semaphores. Data moves between devices by JAX's collectives and lax.ppermute only.
A program may use at most 128 MiB of HBM per device.

```python
import jax
import jax.numpy as jnp
from jax import lax

D = 4096
KW = 31
TOK_DEV = 1024
TOKENS = 16384
N_ROW = 16
N_COL = 8


def raised(drawn, rng, source, target, parts, factor):
    def block_of(position):
        return (jnp.arange(drawn.shape[position]) // (drawn.shape[position] // parts)).reshape((-1,) + (1,) * (drawn.ndim - 1 - position))

    near = jax.random.permutation(rng, parts)[block_of(target)]
    other_side = (block_of(target) + parts // 2) % parts
    return jnp.where((block_of(source) == near) | (block_of(source) == other_side), factor * drawn, drawn)


def level_of(stream_key, dims, split, smallest, top_value):
    factor_of, own = 1.0, jax.random.fold_in(stream_key, 6)
    for axis_at, shards_of in split:
        draws = jnp.exp(jax.random.uniform(jax.random.fold_in(own, axis_at), (shards_of,), jnp.float32, smallest / len(split), top_value / len(split)))
        factor_of = factor_of * jnp.repeat(draws, dims[axis_at] // shards_of).reshape([-1 if axis == axis_at else 1 for axis in range(len(dims))])
    return factor_of


def gaussian(own_key, extent, deviation, bound, shards=(), kind=jnp.bfloat16):
    values = deviation * jax.random.normal(own_key, extent, jnp.float32)
    if shards:
        values = values * level_of(own_key, extent, shards, -0.22, 0.18)
    return jnp.clip(values, -bound, bound).astype(kind)


def bell_draw_with(own_key, dims, spread, reach, shards, heavy, dtype=jnp.bfloat16):
    values = spread * jax.random.normal(own_key, dims, jnp.float32)
    if shards:
        values = values * level_of(own_key, dims, shards, -0.22, 0.18)
    return jnp.clip(raised(values, jax.random.fold_in(own_key, 3), *heavy), -reach, reach).astype(dtype)


def setup_inputs(seed: int = 0) -> dict:
    streams_of = jax.random.split(jax.random.key(seed), 6)
    frames = bell_draw_with(streams_of[0], (TOKENS, D), 1.0, 6.0, ((0, 16), (1, 8)), (0, 1, 16, 2.0))
    w_value = gaussian(streams_of[1], (D, D), D ** -0.5, 0.09375, ((0, 16), (1, 8)))
    w_gate = gaussian(streams_of[2], (D, D), D ** -0.5, 0.09375, ((0, 16), (1, 8)))
    taps = gaussian(streams_of[3], (KW, D), KW ** -0.5, 1.0, ((1, 8),))
    grad_out = gaussian(streams_of[4], (TOKENS, D), 0.5, 4.0, ((0, 16), (1, 8)))
    return {"frames": frames, "w_value": w_value, "w_gate": w_gate, "taps": taps, "grad_out": grad_out}


def reference(frames, w_value, w_gate, taps, grad_out):
    half = (KW - 1) // 2
    kernel = taps.astype(jnp.float32)
    value = jnp.dot(frames, w_value, preferred_element_type=jnp.float32)
    gate = jnp.dot(frames, w_gate, preferred_element_type=jnp.float32)
    gate_prob = jax.nn.sigmoid(gate)
    glu = (value * gate_prob).astype(jnp.bfloat16)
    glu_pad = jnp.pad(glu, ((half, half), (0, 0)))
    filtered = jnp.zeros((TOKENS, D), jnp.float32)
    for k in range(KW):
        filtered = filtered + kernel[k] * glu_pad[k:k + TOKENS].astype(jnp.float32)
    prob = jax.nn.sigmoid(filtered)
    activated = (filtered * prob).astype(jnp.bfloat16)
    grad_filtered = (grad_out.astype(jnp.float32) * (prob + filtered * prob * (1.0 - prob))).astype(jnp.bfloat16)
    grad_pad = jnp.pad(grad_filtered, ((half, half), (0, 0)))
    grad_glu = jnp.zeros((TOKENS, D), jnp.float32)
    for k in range(KW):
        grad_glu = grad_glu + kernel[k] * grad_pad[2 * half - k:2 * half - k + TOKENS].astype(jnp.float32)
    grad_float = grad_filtered.astype(jnp.float32)
    grad_taps = jnp.stack([jnp.sum(grad_float * glu_pad[k:k + TOKENS].astype(jnp.float32), axis=0) for k in range(KW)])
    grad_val = (grad_glu * gate_prob).astype(jnp.bfloat16)
    grad_gt = (grad_glu * value * gate_prob * (1.0 - gate_prob)).astype(jnp.bfloat16)
    width = D // N_COL
    contract = (((1,), (1,)), ((), ()))
    grad_frames = jnp.zeros((TOKENS, D), jnp.float32)
    for block in range(N_COL):
        lo = block * width
        part = lax.dot_general(grad_val[:, lo:lo + width], w_value[:, lo:lo + width], contract, preferred_element_type=jnp.float32)
        part = part + lax.dot_general(grad_gt[:, lo:lo + width], w_gate[:, lo:lo + width], contract, preferred_element_type=jnp.float32)
        grad_frames = grad_frames + part.astype(jnp.bfloat16).astype(jnp.float32)
    both = jnp.concatenate([grad_val, grad_gt], axis=1)
    sums = jnp.zeros((D, 2 * D), jnp.float32)
    for block in range(N_ROW):
        lo = block * TOK_DEV
        term = lax.dot_general(frames[lo:lo + TOK_DEV], both[lo:lo + TOK_DEV], (((0,), (0,)), ((), ())), preferred_element_type=jnp.float32)
        sums = sums + term.astype(jnp.bfloat16).astype(jnp.float32)
    grad_value = sums[:, :D].astype(jnp.bfloat16)
    grad_gate = sums[:, D:].astype(jnp.bfloat16)
    return activated, grad_frames.astype(jnp.bfloat16), grad_value, grad_gate, grad_taps
```

```python
import jax
import jax.numpy as jnp
from jax import lax
from jax.sharding import PartitionSpec as P

F32 = jnp.float32
BF16 = jnp.bfloat16
BOTH = ("row", "col")
RING = 4
CORES = 2


def moves(step):
    pairs = []
    for z in range(RING):
        for y in range(RING):
            for x in range(RING):
                for core in range(CORES):
                    tz, ty, tx, tc = step(z, y, x, core)
                    source = ((z * RING + y) * RING + x) * CORES + core
                    target = ((tz % RING * RING + ty % RING) * RING + tx % RING) * CORES + tc
                    pairs.append((source, target))
    return pairs


def way(core):
    return 1 - 2 * core


ALONG_X = moves(lambda z, y, x, core: (z, y, x + way(core), core))
ALONG_Y = moves(lambda z, y, x, core: (z, y + way(core), x, core))
ALONG_Z = moves(lambda z, y, x, core: (z + way(core), y, x, core))
SIBLING = moves(lambda z, y, x, core: (z, y, x, 1 - core))


def send(array, pairs):
    return lax.ppermute(array, BOTH, pairs)


def dot(a, b, dims):
    return lax.dot_general(a, b, (dims, ((), ())), preferred_element_type=F32)


def padded(array, width):
    count, length = lax.axis_size("row"), array.shape[0]
    up = [(i, i + 1) for i in range(count - 1)]
    down = [(j, i) for i, j in up]
    before = lax.ppermute(array[length - width :], "row", up)
    after = lax.ppermute(array[:width], "row", down)
    return jnp.concatenate([before, array, after], axis=0)


def per_device(frames, w_value, w_gate, taps, grad_out):
    width = taps.shape[0]
    half = (width - 1) // 2
    kernel = taps.astype(F32)
    rows, part = frames.shape
    depth, channels = w_value.shape
    row, col = lax.axis_index("row"), lax.axis_index("col")
    z, y = row // RING, row % RING
    x, core = col // CORES, col % CORES
    turn = way(core)

    def at(place, step):
        return (place + step * turn) % RING

    whole_t = jnp.zeros((RING * CORES, part, rows), BF16)
    whole = jnp.zeros((rows, RING * CORES * part), BF16)
    full_value = jnp.zeros((RING, RING * depth, channels), BF16)
    full_gate = jnp.zeros((RING, RING, depth, channels), BF16)
    value_plane = jnp.zeros((RING, depth, channels), BF16)
    gate_plane = jnp.zeros((RING, depth, channels), BF16)
    block, v, g = frames, w_value, w_gate
    for step in range(RING):
        value_plane = lax.dynamic_update_slice(value_plane, v[None], (at(y, -step), 0, 0))
        gate_plane = lax.dynamic_update_slice(gate_plane, g[None], (at(z, -step), 0, 0))
        if step < RING - 1:
            v, g = send(v, ALONG_Y), send(g, ALONG_Z)
    v, g = value_plane.reshape(RING * depth, channels), gate_plane
    for step in range(RING):
        other = send(block, SIBLING)
        mine = at(x, -step) * CORES + core
        theirs = at(x, step) * CORES + 1 - core
        whole = lax.dynamic_update_slice(whole, block, (0, mine * part))
        whole = lax.dynamic_update_slice(whole, other, (0, theirs * part))
        whole_t = lax.dynamic_update_slice(whole_t, block.T[None], (mine, 0, 0))
        whole_t = lax.dynamic_update_slice(whole_t, other.T[None], (theirs, 0, 0))
        full_value = lax.dynamic_update_slice(full_value, v[None], (at(z, -step), 0, 0))
        full_gate = lax.dynamic_update_slice(full_gate, g[:, None], (0, at(y, -step), 0, 0))
        if step < RING - 1:
            block, v, g = send(block, ALONG_X), send(v, ALONG_Z), send(g, ALONG_Y)
    full_value = full_value.reshape(-1, channels)
    full_gate = full_gate.reshape(-1, channels)

    value = dot(whole, full_value, ((1,), (0,)))
    gate = dot(whole, full_gate, ((1,), (0,)))
    gate_prob = jax.nn.sigmoid(gate)
    glu = (value * gate_prob).astype(BF16)
    glu_pad = padded(glu, half)
    filtered = jnp.zeros((rows, channels), F32)
    for k in range(width):
        filtered = filtered + kernel[k] * glu_pad[k : k + rows].astype(F32)
    prob = jax.nn.sigmoid(filtered)
    activated = (filtered * prob).astype(BF16)
    grad_filtered = (grad_out.astype(F32) * (prob + filtered * prob * (1.0 - prob))).astype(BF16)
    grad_pad = padded(grad_filtered, half)
    grad_glu = jnp.zeros((rows, channels), F32)
    for k in range(width):
        grad_glu = grad_glu + kernel[k] * grad_pad[2 * half - k : 2 * half - k + rows].astype(F32)
    grad_float = grad_filtered.astype(F32)
    tap_sum = jnp.stack(
        [jnp.sum(grad_float * glu_pad[k : k + rows].astype(F32), axis=0) for k in range(width)]
    )
    grad_val = (grad_glu * gate_prob).astype(BF16)
    grad_gt = (grad_glu * value * gate_prob * (1.0 - gate_prob)).astype(BF16)

    def frames_part(place, side):
        start = (place * CORES + side) * part
        block_v = lax.dynamic_slice_in_dim(full_value, start, part, 0)
        block_g = lax.dynamic_slice_in_dim(full_gate, start, part, 0)
        return dot(grad_val, block_v, ((1,), (1,))) + dot(grad_gt, block_g, ((1,), (1,)))

    whole_t = whole_t.reshape(RING, RING, depth, rows)

    def value_part(place):
        left = lax.dynamic_slice_in_dim(whole_t, place, 1, 0).reshape(RING * depth, rows)
        return dot(left, grad_val, ((1,), (0,)))

    def gate_part(place):
        left = lax.dynamic_slice_in_dim(whole_t, place, 1, 1).reshape(RING * depth, rows)
        return dot(left, grad_gt, ((1,), (0,)))

    got_f = got_v = got_g = None
    for step in range(1, RING + 1):
        there = send(frames_part(at(x, step), 1 - core).astype(BF16), SIBLING)
        sum_v = value_part(at(z, -step))
        sum_g = gate_part(at(y, -step))
        sum_f = frames_part(at(x, -step), core) + there.astype(F32)
        if step > 1:
            sum_v, sum_g, sum_f = (
                sum_v + got_v.astype(F32),
                sum_g + got_g.astype(F32),
                sum_f + got_f.astype(F32),
            )
        if step < RING:
            got_v = send(sum_v.astype(BF16), ALONG_Z)
            got_g = send(sum_g.astype(BF16), ALONG_Y)
            got_f = send(sum_f.astype(BF16), ALONG_X)
    grad_frames = sum_f.astype(BF16)
    sum_v = sum_v.reshape(RING, depth, channels)
    sum_g = sum_g.reshape(RING, depth, channels)
    for step in range(1, RING + 1):
        part_v = lax.dynamic_index_in_dim(sum_v, at(y, -step), 0, keepdims=False)
        part_g = lax.dynamic_index_in_dim(sum_g, at(z, -step), 0, keepdims=False)
        if step > 1:
            part_v, part_g = part_v + got_v.astype(F32), part_g + got_g.astype(F32)
        if step < RING:
            got_v = send(part_v.astype(BF16), ALONG_Y)
            got_g = send(part_g.astype(BF16), ALONG_Z)
    grad_value, grad_gate = part_v.astype(BF16), part_g.astype(BF16)
    count, stride = lax.axis_size("row"), 1
    while stride < count:
        tap_sum = tap_sum + lax.ppermute(tap_sum, "row", [(i, i ^ stride) for i in range(count)])
        stride *= 2
    return (activated, grad_frames, grad_value, grad_gate, tap_sum)


def solution(mesh):
    in_specs = (P("row", "col"), P("row", "col"), P("row", "col"), P(None, "col"), P("row", "col"))
    out_specs = (P("row", "col"), P("row", "col"), P("row", "col"), P("row", "col"), P(None, "col"))
    return jax.shard_map(
        per_device, mesh=mesh, in_specs=in_specs, out_specs=out_specs, check_vma=False
    )
```

```python
import functools

import jax
import jax.numpy as jnp
from jax import lax
from jax.experimental import pallas as pl
from jax.experimental.pallas import tpu as pltpu
from jax.sharding import PartitionSpec as P

F32 = jnp.float32
BF16 = jnp.bfloat16
BOTH = ("row", "col")
RING = 4
CORES = 2


def moves(step):
    pairs = []
    for z in range(RING):
        for y in range(RING):
            for x in range(RING):
                for core in range(CORES):
                    tz, ty, tx, tc = step(z, y, x, core)
                    source = ((z * RING + y) * RING + x) * CORES + core
                    target = ((tz % RING * RING + ty % RING) * RING + tx % RING) * CORES + tc
                    pairs.append((source, target))
    return pairs


def way(core):
    return 1 - 2 * core


ALONG_X = moves(lambda z, y, x, core: (z, y, x + way(core), core))
ALONG_Y = moves(lambda z, y, x, core: (z, y + way(core), x, core))
ALONG_Z = moves(lambda z, y, x, core: (z + way(core), y, x, core))
SIBLING = moves(lambda z, y, x, core: (z, y, x, 1 - core))


def send(array, pairs):
    return lax.ppermute(array, BOTH, pairs)


def dot(a, b, dims):
    return lax.dot_general(a, b, (dims, ((), ())), preferred_element_type=F32)


def padded(array, width):
    count, length = lax.axis_size("row"), array.shape[0]
    up = [(i, i + 1) for i in range(count - 1)]
    down = [(j, i) for i, j in up]
    before = lax.ppermute(array[length - width :], "row", up)
    after = lax.ppermute(array[:width], "row", down)
    return jnp.concatenate([before, array, after], axis=0)


EDGE=32
LANES=128
STRIP=32

def middle_body(width, whole, wv, wg, gout, taps, act, gval, ggt, gtap, vg, glu, gf, gp_s, vs_s):
    half=(width-1)//2
    total=whole.shape[0]
    rows=total-2*EDGE
    w=jnp.concatenate([wv[...],wg[...]],axis=1)
    vg[...]=jnp.dot(whole[...],w,preferred_element_type=F32)
    def gates(i,_):
        at=pl.ds(pl.multiple_of(i*STRIP,STRIP),STRIP)
        v=vg[at,:LANES]; p=jax.nn.sigmoid(vg[at,LANES:])
        vp=v*p
        glu[at,:]=vp.astype(BF16).astype(F32)
        gp_s[at,:]=p
        vs_s[at,:]=vp*(1.0-p)
        return 0
    lax.fori_loop(0,total//STRIP,gates,0)
    tap=[jnp.broadcast_to(taps[k:k+1,:],(8,LANES)) for k in range(width)]
    def conv(src,start,sign):
        parts=[jnp.zeros((8,LANES),F32) for _ in range(STRIP//8)]
        for k in range(width):
            off=k-half if sign>0 else half-k
            x=src[pl.ds(start+off,STRIP),:]
            for j in range(STRIP//8):
                parts[j]=parts[j]+tap[k]*x[8*j:8*j+8]
        return jnp.concatenate(parts,axis=0)
    gf[0:EDGE,:]=jnp.zeros((EDGE,LANES),F32)
    gf[total-EDGE:total,:]=jnp.zeros((EDGE,LANES),F32)
    def forward(i,_):
        start=pl.multiple_of(i*STRIP,16)+EDGE//2
        at=pl.ds(start,STRIP)
        f=conv(glu,start,1)
        s=jax.nn.sigmoid(f)
        fs=f*s
        vg[at,:LANES]=fs
        g=gout[at,:].astype(F32)*(s+fs*(1.0-s))
        gf[at,:]=g.astype(BF16).astype(F32)
        return 0
    lax.fori_loop(0,(rows+EDGE)//STRIP,forward,0)
    act[...]=vg[EDGE:EDGE+rows,:LANES].astype(BF16)
    def backward(i,_):
        start=pl.multiple_of(i*STRIP,STRIP)
        at=pl.ds(start,STRIP)
        src=pl.ds(start+EDGE,STRIP)
        d=conv(gf,start+EDGE,-1)
        gval[at,:]=(d*gp_s[src,:]).astype(BF16)
        ggt[at,:]=(d*vs_s[src,:]).astype(BF16)
        return 0
    lax.fori_loop(0,rows//STRIP,backward,0)
    def tapsum(i,acc):
        start=pl.multiple_of(i*STRIP,STRIP)+EDGE
        q=gf[pl.ds(start,STRIP),:]
        out=[]
        for k in range(width):
            x=glu[pl.ds(start+k-half,STRIP),:]*q
            t=acc[k]
            for j in range(STRIP//8): t=t+x[8*j:8*j+8]
            out.append(t)
        return tuple(out)
    acc=lax.fori_loop(0,rows//STRIP,tapsum,tuple(jnp.zeros((8,LANES),F32) for _ in range(width)))
    for k in range(width):
        gtap[k:k+1,:]=jnp.sum(acc[k],axis=0,keepdims=True)
    gtap[width:,:]=jnp.zeros((gtap.shape[0]-width,LANES),F32)

def middle(whole, full_value, full_gate, gout, taps):
    total,inner=whole.shape
    channels=full_value.shape[1]
    rows=total-2*EDGE
    width=taps.shape[0]
    tall=-(-width//8)*8
    tapf=jnp.pad(taps.astype(F32),((0,tall-width),(0,0)))
    col=lambda n:pl.BlockSpec((n,LANES),lambda j:(0,j))
    sds=jax.ShapeDtypeStruct
    return pl.pallas_call(
        functools.partial(middle_body,width),
        grid=(channels//LANES,),
        in_specs=[pl.BlockSpec((total,inner),lambda j:(0,0),pipeline_mode=pl.Buffered(1)),col(inner),col(inner),col(total),col(tall)],
        out_specs=[col(rows),col(rows),col(rows),col(tall)],
        out_shape=[sds((rows,channels),BF16)]*3+[sds((tall,channels),F32)],
        scratch_shapes=[pltpu.VMEM((total,2*LANES),F32)]+[pltpu.VMEM((total,LANES),F32)]*4,
        compiler_params=pltpu.CompilerParams(vmem_limit_bytes=56*2**20),
    )(whole,full_value,full_gate,gout,tapf)


def per_device(frames, w_value, w_gate, taps, grad_out):
    width = taps.shape[0]
    rows, part = frames.shape
    depth, channels = w_value.shape
    row, col = lax.axis_index("row"), lax.axis_index("col")
    z, y = row // RING, row % RING
    x, core = col // CORES, col % CORES
    turn = way(core)

    def at(place, step):
        return (place + step * turn) % RING

    whole_t = jnp.zeros((RING * CORES, part, rows), BF16)
    frames_wide, grad_wide = padded(frames, EDGE), padded(grad_out, EDGE)
    whole = jnp.zeros((rows + 2 * EDGE, RING * CORES * part), BF16)
    full_value = jnp.zeros((RING, RING * depth, channels), BF16)
    full_gate = jnp.zeros((RING, RING, depth, channels), BF16)
    value_plane = jnp.zeros((RING, depth, channels), BF16)
    gate_plane = jnp.zeros((RING, depth, channels), BF16)
    block, v, g = frames_wide, w_value, w_gate
    for step in range(RING):
        value_plane = lax.dynamic_update_slice(value_plane, v[None], (at(y, -step), 0, 0))
        gate_plane = lax.dynamic_update_slice(gate_plane, g[None], (at(z, -step), 0, 0))
        if step < RING - 1:
            v, g = send(v, ALONG_Y), send(g, ALONG_Z)
    v, g = value_plane.reshape(RING * depth, channels), gate_plane
    for step in range(RING):
        other = send(block, SIBLING)
        mine = at(x, -step) * CORES + core
        theirs = at(x, step) * CORES + 1 - core
        whole = lax.dynamic_update_slice(whole, block, (0, mine * part))
        whole = lax.dynamic_update_slice(whole, other, (0, theirs * part))
        whole_t = lax.dynamic_update_slice(whole_t, block[EDGE : EDGE + rows].T[None], (mine, 0, 0))
        whole_t = lax.dynamic_update_slice(whole_t, other[EDGE : EDGE + rows].T[None], (theirs, 0, 0))
        full_value = lax.dynamic_update_slice(full_value, v[None], (at(z, -step), 0, 0))
        full_gate = lax.dynamic_update_slice(full_gate, g[:, None], (0, at(y, -step), 0, 0))
        if step < RING - 1:
            block, v, g = send(block, ALONG_X), send(v, ALONG_Z), send(g, ALONG_Y)
    full_value = full_value.reshape(-1, channels)
    full_gate = full_gate.reshape(-1, channels)

    activated, grad_val, grad_gt, tap_sum = middle(whole, full_value, full_gate, grad_wide, taps)
    tap_sum = tap_sum[:width]

    def frames_part(place, side):
        start = (place * CORES + side) * part
        block_v = lax.dynamic_slice_in_dim(full_value, start, part, 0)
        block_g = lax.dynamic_slice_in_dim(full_gate, start, part, 0)
        return dot(grad_val, block_v, ((1,), (1,))) + dot(grad_gt, block_g, ((1,), (1,)))

    whole_t = whole_t.reshape(RING, RING, depth, rows)

    def value_part(place):
        left = lax.dynamic_slice_in_dim(whole_t, place, 1, 0).reshape(RING * depth, rows)
        return dot(left, grad_val, ((1,), (0,)))

    def gate_part(place):
        left = lax.dynamic_slice_in_dim(whole_t, place, 1, 1).reshape(RING * depth, rows)
        return dot(left, grad_gt, ((1,), (0,)))

    got_f = got_v = got_g = None
    for step in range(1, RING + 1):
        there = send(frames_part(at(x, step), 1 - core).astype(BF16), SIBLING)
        sum_v = value_part(at(z, -step))
        sum_g = gate_part(at(y, -step))
        sum_f = frames_part(at(x, -step), core) + there.astype(F32)
        if step > 1:
            sum_v, sum_g, sum_f = (
                sum_v + got_v.astype(F32),
                sum_g + got_g.astype(F32),
                sum_f + got_f.astype(F32),
            )
        if step < RING:
            got_v = send(sum_v.astype(BF16), ALONG_Z)
            got_g = send(sum_g.astype(BF16), ALONG_Y)
            got_f = send(sum_f.astype(BF16), ALONG_X)
    grad_frames = sum_f.astype(BF16)
    sum_v = sum_v.reshape(RING, depth, channels)
    sum_g = sum_g.reshape(RING, depth, channels)
    for step in range(1, RING + 1):
        part_v = lax.dynamic_index_in_dim(sum_v, at(y, -step), 0, keepdims=False)
        part_g = lax.dynamic_index_in_dim(sum_g, at(z, -step), 0, keepdims=False)
        if step > 1:
            part_v, part_g = part_v + got_v.astype(F32), part_g + got_g.astype(F32)
        if step < RING:
            got_v = send(part_v.astype(BF16), ALONG_Y)
            got_g = send(part_g.astype(BF16), ALONG_Z)
    grad_value, grad_gate = part_v.astype(BF16), part_g.astype(BF16)
    count, stride = lax.axis_size("row"), 1
    while stride < count:
        tap_sum = tap_sum + lax.ppermute(tap_sum, "row", [(i, i ^ stride) for i in range(count)])
        stride *= 2
    return (activated, grad_frames, grad_value, grad_gate, tap_sum)


def solution(mesh):
    in_specs = (P("row", "col"), P("row", "col"), P("row", "col"), P(None, "col"), P("row", "col"))
    out_specs = (P("row", "col"), P("row", "col"), P("row", "col"), P("row", "col"), P(None, "col"))
    return jax.shard_map(
        per_device, mesh=mesh, in_specs=in_specs, out_specs=out_specs, check_vma=False
    )
```

```python
import functools

import jax
import jax.numpy as jnp
from jax import lax
from jax.experimental import pallas as pl
from jax.experimental.pallas import tpu as pltpu
from jax.sharding import PartitionSpec as P

F32 = jnp.float32
BF16 = jnp.bfloat16
BOTH = ("row", "col")
RING = 4
CORES = 2
EDGE = 32
LANES = 128
STRIP = 32
MIB = 2**20


def turning(step):
    pairs = []
    for source in range(RING * RING * RING * CORES):
        rest, core = source // CORES, source % CORES
        at = [rest // RING**2, rest // RING % RING, rest % RING]
        at, core = step(at, core)
        z, y, x = (place % RING for place in at)
        pairs.append((source, ((z * RING + y) * RING + x) * CORES + core))
    return pairs


def way(core):
    return 1 - 2 * core


ALONG_Y = turning(lambda at, core: ((at[0], at[1] + way(core), at[2]), core))
ALONG_Z = turning(lambda at, core: ((at[0] + way(core), at[1], at[2]), core))
BACK_Y = turning(lambda at, core: ((at[0], at[1] - way(core), at[2]), core))
BACK_Z = turning(lambda at, core: ((at[0] - way(core), at[1], at[2]), core))
TWO_Y = turning(lambda at, core: ((at[0], at[1] + 2, at[2]), core))
TWO_Z = turning(lambda at, core: ((at[0] + 2, at[1], at[2]), core))
UP_Y = turning(lambda at, core: ((at[0], at[1] + 1, at[2]), core))
UP_Z = turning(lambda at, core: ((at[0] + 1, at[1], at[2]), core))
DOWN_Y = turning(lambda at, core: ((at[0], at[1] - 1, at[2]), core))
DOWN_Z = turning(lambda at, core: ((at[0] - 1, at[1], at[2]), core))
OFFSETS = (0, -1, 1, 2)


def send(array, pairs):
    return lax.ppermute(array, BOTH, pairs)


def halo(array):
    count, length = lax.axis_size("row"), array.shape[0]
    up = [(i, i + 1) for i in range(count - 1)]
    down = [(j, i) for i, j in up]
    before = lax.ppermute(array[length - EDGE :], "row", up)
    after = lax.ppermute(array[:EDGE], "row", down)
    return before, after


def together(*values):
    return lax.optimization_barrier(values)


def middle_body(width, rows, place, *refs):
    pieces, (before, inner, after), (gout, taps) = refs[:10], refs[10:13], refs[13:15]
    act, turned_both, frames_out, first_out, gtap = refs[15:20]
    vg, glu, gf, gate_s, vg_s, both, whole, weights, in_sem = refs[20:]
    half = (width - 1) // 2
    total = whole.shape[0]
    depth, channels = weights.shape[1], weights.shape[2] // 2
    strip = pl.program_id(0)
    strips = channels // LANES
    z, y, turn = place[0], place[1], place[2]
    copies = [
        (before, whole.at[pl.ds(0, EDGE), :]),
        (inner, whole.at[pl.ds(EDGE, rows), :]),
        (after, whole.at[pl.ds(EDGE + rows, EDGE), :]),
    ]
    for kind in range(2):
        for far in range(RING):
            for near in range(RING):
                if far < RING - 1:
                    source = pieces[5 * kind + far].at[near]
                else:
                    source = pieces[5 * kind + far + near // 2].at[near % 2]
                a, b = (near, far) if kind else (far, near)
                row = lax.rem(z + OFFSETS[a] + RING, RING) * RING
                row = row + lax.rem(y + OFFSETS[b] + RING, RING)
                copies.append((source, weights.at[row, :, pl.ds(kind * channels, channels)]))
    copies = [
        pltpu.make_async_copy(source, target, in_sem.at[n])
        for n, (source, target) in enumerate(copies)
    ]
    @pl.when(strip == 0)
    def _():
        for copy in copies:
            copy.start()
        for copy in copies:
            copy.wait()

    @pl.when(strip < strips)
    def _():
        def columns(kind):
            start = pl.multiple_of(kind * channels + strip * LANES, LANES)
            return weights[:, :, pl.ds(start, LANES)].reshape(RING * RING * depth, LANES)

        vg[...] = jnp.dot(
            whole[...], jnp.concatenate([columns(0), columns(1)], axis=1), preferred_element_type=F32
        )

        def gates(i, _):
            at = pl.ds(pl.multiple_of(i * STRIP, STRIP), STRIP)
            p = jax.nn.sigmoid(vg[at, LANES:])
            vp = vg[at, :LANES] * p
            glu[at, :] = vp.astype(BF16).astype(F32)
            gate_s[at, :] = p
            vg_s[at, :] = vp * (1.0 - p)
            return 0

        lax.fori_loop(0, total // STRIP, gates, 0)
        tap = [jnp.broadcast_to(taps[k : k + 1, :], (8, LANES)) for k in range(width)]

        def conv(source, start, sign):
            parts = [jnp.zeros((8, LANES), F32) for _ in range(STRIP // 8)]
            for k in range(width):
                x = source[pl.ds(start + sign * (k - half), STRIP), :]
                for j in range(STRIP // 8):
                    parts[j] = parts[j] + tap[k] * x[8 * j : 8 * j + 8]
            return jnp.concatenate(parts, axis=0)

        gf[0:EDGE, :] = jnp.zeros((EDGE, LANES), F32)
        gf[total - EDGE : total, :] = jnp.zeros((EDGE, LANES), F32)

        def forward(i, _):
            start = pl.multiple_of(i * STRIP, 16) + EDGE // 2
            at = pl.ds(start, STRIP)
            f = conv(glu, start, 1)
            s = jax.nn.sigmoid(f)
            fs = f * s
            vg[at, :LANES] = fs
            g = gout[at, :].astype(F32) * (s + fs * (1.0 - s))
            gf[at, :] = g.astype(BF16).astype(F32)
            return 0

        lax.fori_loop(0, (rows + EDGE) // STRIP, forward, 0)
        act[...] = vg[EDGE : EDGE + rows, :LANES].astype(BF16)

        def backward(i, _):
            start = pl.multiple_of(i * STRIP, STRIP) + EDGE
            at = pl.ds(start, STRIP)
            d = conv(gf, start, -1)
            vg[at, :LANES] = d * gate_s[at, :]
            vg[at, LANES:] = d * vg_s[at, :]
            return 0

        lax.fori_loop(0, rows // STRIP, backward, 0)
        for kind in range(2):
            grad = vg[EDGE : EDGE + rows, kind * LANES : (kind + 1) * LANES]
            start = pl.multiple_of(kind * channels + strip * LANES, LANES)
            both[:, pl.ds(start, LANES)] = grad.astype(BF16)
            turned_both[kind, pl.ds(pl.multiple_of(strip * LANES, LANES), LANES), :] = grad.T.astype(
                BF16
            )

        def tap_sums(i, total_sums):
            start = pl.multiple_of(i * STRIP, STRIP) + EDGE
            q = gf[pl.ds(start, STRIP), :]
            out = []
            for k in range(width):
                x = glu[pl.ds(start + k - half, STRIP), :] * q
                t = total_sums[k]
                for j in range(STRIP // 8):
                    t = t + x[8 * j : 8 * j + 8]
                out.append(t)
            return tuple(out)

        start_sums = tuple(jnp.zeros((8, LANES), F32) for _ in range(width))
        sums = lax.fori_loop(0, rows // STRIP, tap_sums, start_sums)
        for k in range(width):
            gtap[k : k + 1, :] = jnp.sum(sums[k], axis=0, keepdims=True)
        gtap[width:, :] = jnp.zeros((gtap.shape[0] - width, LANES), F32)

    @pl.when((strip >= strips) & (strip < strips + RING * CORES))
    def _():
        block = weights[pl.ds((strip - strips) * CORES, CORES)].reshape(-1, 2 * channels)
        frames_out[...] = lax.dot_general(
            both[...], block, (((1,), (1,)), ((), ())), preferred_element_type=F32
        ).astype(BF16)

    for kind in range(2):

        @pl.when(strip == strips + RING * CORES + kind)
        def _():
            for q in range(RING):
                far = lax.rem(y + RING - turn, RING) if kind else lax.rem(z + RING - turn, RING)
                near = (z if kind else y) + 2 * RING - (q + 1) * turn
                near = lax.rem(near, RING)
                row = near * RING + far if kind else far * RING + near
                part = whole[EDGE : EDGE + rows, pl.ds(pl.multiple_of(row * depth, LANES), depth)]
                first_out[0, q] = jnp.dot(
                    turned_both[kind], part, preferred_element_type=F32
                ).astype(BF16)


def middle(place, pieces, parts, gout, taps):
    rows, inner = parts[1].shape
    total = rows + 2 * EDGE
    depth, channels = pieces[0].shape[1:]
    width = taps.shape[0]
    tall = -(-width // 8) * 8
    taps = jnp.pad(taps.astype(F32), ((0, tall - width), (0, 0)))

    def strips(n):
        return pl.BlockSpec((n, LANES), lambda j, place: (0, jnp.minimum(j, count - 1)))

    def far():
        return pl.BlockSpec(memory_space=pltpu.HBM)

    count = channels // LANES
    part = inner // (RING * CORES)
    begin, end = count, count + RING * CORES

    def frames_block(j, place):
        return (0, jnp.clip(j - begin, 0, RING * CORES - 1))

    def first_block(j, place):
        return (jnp.maximum(j - end, 0), 0, 0, 0)

    shape = jax.ShapeDtypeStruct
    return pl.pallas_call(
        functools.partial(middle_body, width, rows),
        grid_spec=pltpu.PrefetchScalarGridSpec(
            num_scalar_prefetch=1,
            grid=(end + 2,),
            in_specs=[far() for _ in range(len(pieces) + len(parts))] + [strips(total), strips(tall)],
            out_specs=[
                strips(rows),
                pl.BlockSpec((2, channels, rows), lambda j, place: (0, 0, 0)),
                pl.BlockSpec((rows, part), frames_block),
                pl.BlockSpec((1, RING, channels, depth), first_block),
                strips(tall),
            ],
            scratch_shapes=[pltpu.VMEM((total, 2 * LANES), F32)]
            + [pltpu.VMEM((total, LANES), F32)] * 4
            + [
                pltpu.VMEM((rows, 2 * channels), BF16),
                pltpu.VMEM((total, inner), BF16),
                pltpu.VMEM((RING * RING, depth, 2 * channels), BF16),
                pltpu.SemaphoreType.DMA((2 * RING * RING + 3,)),
            ],
        ),
        out_shape=[
            shape((rows, channels), BF16),
            shape((2, channels, rows), BF16),
            shape((rows, inner), BF16),
            shape((2, RING, channels, depth), BF16),
            shape((tall, channels), F32),
        ],
        compiler_params=pltpu.CompilerParams(vmem_limit_bytes=60 * MIB),
        cost_estimate=pl.CostEstimate(
            flops=40 * 10**9, bytes_accessed=40 * MIB, transcendentals=0
        ),
    )(place, *pieces, *parts, gout, taps)


def weight_body(order, grad, a, b, c, d, out):
    for q, part in enumerate((a, b, c, d)):
        out[0, q] = jnp.dot(grad[0], part[...], preferred_element_type=F32).astype(BF16)


def weight_parts(order, turned_both, whole, depth):
    kinds, channels, rows = turned_both.shape
    count = order.shape[0]

    def block(q):
        return pl.BlockSpec((rows, depth), lambda i, order: (0, order[i, q + 1]))

    return pl.pallas_call(
        weight_body,
        grid_spec=pltpu.PrefetchScalarGridSpec(
            num_scalar_prefetch=1,
            grid=(count,),
            in_specs=[pl.BlockSpec((1, channels, rows), lambda i, order: (order[i, 0], 0, 0))]
            + [block(q) for q in range(RING)],
            out_specs=pl.BlockSpec((1, RING, channels, depth), lambda i, order: (i, 0, 0, 0)),
        ),
        out_shape=jax.ShapeDtypeStruct((count, RING, channels, depth), BF16),
        compiler_params=pltpu.CompilerParams(vmem_limit_bytes=60 * MIB),
        cost_estimate=pl.CostEstimate(
            flops=count * RING * 2 * channels * depth * rows,
            bytes_accessed=count * 4 * MIB,
            transcendentals=0,
        ),
    )(order, turned_both, *[whole] * RING)


def plus(a, *others):
    total = a.astype(F32)
    for other in others:
        total = total + other.astype(F32)
    return total.astype(BF16)


def spread(block, up, down):
    cut = block.shape[0] // 2
    below, above = send(block, up), send(block, down)
    return [block, below, above, send(below[:cut], up), send(above[cut:], down)]


def per_device(frames, w_value, w_gate, taps, grad_out):
    width = taps.shape[0]
    row, col = lax.axis_index("row"), lax.axis_index("col")
    z, y = row // RING, row % RING
    depth = w_value.shape[0]
    turn = way(col % CORES)

    whole = lax.all_gather(frames, "col", axis=1, tiled=True)
    value, gate = spread(w_value, UP_Y, DOWN_Y), spread(w_gate, UP_Z, DOWN_Z)
    grad_out, *near = together(grad_out, *value, *gate)
    value, gate = near[:5], near[5:]
    shape = (RING,) + w_value.shape
    value = jnp.concatenate(value).reshape(shape)
    gate = jnp.concatenate(gate).reshape(shape)
    pieces = spread(value, UP_Z, DOWN_Z) + spread(gate, UP_Y, DOWN_Y)
    before, after = halo(grad_out)
    grad_wide = jnp.concatenate([before, grad_out, after], axis=0)
    before, after = halo(whole)
    place = jnp.stack([z, y, turn]).astype(jnp.int32)
    activated, turned_both, part, first, tap_sum = middle(
        place, pieces, (before, whole, after), grad_wide, taps
    )

    def behind(at, step):
        return (at - step * turn) % RING

    def of_weights(step):
        sides = [1, 2, 3, 4]
        value = [0] + [behind(z, step) * RING + behind(y, q) for q in sides]
        gate = [1] + [behind(z, q) * RING + behind(y, step) for q in sides]
        return [value, gate]

    def table(rows):
        return jnp.array(rows, jnp.int32)

    grad_frames = lax.psum_scatter(part, "col", scatter_dimension=1, tiled=True)

    def folded(stride):
        pairs = [(i, i ^ stride) for i in range(RING * RING)]
        return tap_sum + lax.ppermute(tap_sum, "row", pairs)

    tap_sum = folded(1)
    order = of_weights(2) + of_weights(3) + of_weights(4)
    later = weight_parts(table(order), turned_both, whole, depth)
    later, tap_sum = together(later, tap_sum)

    def shares(step, group):
        cut = slice(2 * group, 2 * group + 2)
        if step == 1:
            return first[0, cut], first[1, cut]
        return later[(step - 2) * 2, cut], later[(step - 2) * 2 + 1, cut]

    def onward(held):
        return send(held[0], ALONG_Z), send(held[1], ALONG_Y)

    moving = [onward(shares(1, 0)), onward(shares(1, 1))]
    last = None
    for step in range(2, RING + 1):
        for group in range(2):
            got = moving[group]
            if last is not None:
                got = together(*got, *last)[:2]
            last = tuple(plus(a, b) for a, b in zip(shares(step, group), got))
            moving[group] = onward(last) if step < RING else last
        if step < RING:
            *last, tap_sum = together(*last, tap_sum)
            tap_sum = folded(2 ** (step - 1))
            tap_sum, *moving[0] = together(tap_sum, *moving[0])
    tap_sum, *moving[0] = together(tap_sum, *moving[0])
    tap_sum = folded(8)
    near = [
        (send(moving[0][kind][0], along), send(moving[0][kind][1], two))
        for kind, along, two in ((0, BACK_Y, TWO_Y), (1, BACK_Z, TWO_Z))
    ]
    grads = []
    for kind, pairs in ((0, ALONG_Y), (1, ALONG_Z)):
        got = send(moving[1][kind][0], pairs)
        grads.append(plus(moving[1][kind][1], *near[kind], got).T)
    return (activated, grad_frames, *grads, tap_sum[:width])


def solution(mesh):
    in_specs = (P("row", "col"), P("row", "col"), P("row", "col"), P(None, "col"), P("row", "col"))
    out_specs = (P("row", "col"), P("row", "col"), P("row", "col"), P("row", "col"), P(None, "col"))
    return jax.shard_map(
        per_device, mesh=mesh, in_specs=in_specs, out_specs=out_specs, check_vma=False
    )
```

```python
import functools

import jax
import jax.numpy as jnp
from jax import lax
from jax.experimental import pallas as pl
from jax.experimental.pallas import tpu as pltpu
from jax.sharding import PartitionSpec as P

F32 = jnp.float32
BF16 = jnp.bfloat16
BOTH = ("row", "col")
RING = 4
CORES = 2
EDGE = 32
LANES = 128
STRIP = 32
MIB = 2**20


def turning(step):
    pairs = []
    for source in range(RING * RING * RING * CORES):
        rest, core = source // CORES, source % CORES
        at = [rest // RING**2, rest // RING % RING, rest % RING]
        at, core = step(at, core)
        z, y, x = (place % RING for place in at)
        pairs.append((source, ((z * RING + y) * RING + x) * CORES + core))
    return pairs


def way(core):
    return 1 - 2 * core


ALONG_Y = turning(lambda at, core: ((at[0], at[1] + way(core), at[2]), core))
ALONG_Z = turning(lambda at, core: ((at[0] + way(core), at[1], at[2]), core))
BACK_Y = turning(lambda at, core: ((at[0], at[1] - way(core), at[2]), core))
BACK_Z = turning(lambda at, core: ((at[0] - way(core), at[1], at[2]), core))
TWO_Y = turning(lambda at, core: ((at[0], at[1] + 2, at[2]), core))
TWO_Z = turning(lambda at, core: ((at[0] + 2, at[1], at[2]), core))
UP_Y = turning(lambda at, core: ((at[0], at[1] + 1, at[2]), core))
UP_Z = turning(lambda at, core: ((at[0] + 1, at[1], at[2]), core))
DOWN_Y = turning(lambda at, core: ((at[0], at[1] - 1, at[2]), core))
DOWN_Z = turning(lambda at, core: ((at[0] - 1, at[1], at[2]), core))
OFFSETS = (0, -1, 1, 2)


def send(array, pairs):
    return lax.ppermute(array, BOTH, pairs)


def halo(*arrays):
    count, length = lax.axis_size("row"), arrays[0].shape[0]
    up = [(i, i + 1) for i in range(count - 1)]
    down = [(j, i) for i, j in up]
    last = jnp.concatenate([array[length - EDGE :] for array in arrays], axis=1)
    first = jnp.concatenate([array[:EDGE] for array in arrays], axis=1)
    return lax.ppermute(last, "row", up), lax.ppermute(first, "row", down)


def together(*values):
    return lax.optimization_barrier(values)


def middle_body(width, rows, place, *refs):
    pieces, (before, inner, after, grad_out), taps = refs[:10], refs[10:14], refs[14]
    act, turned_both, frames_out, first_out, gtap = refs[15:20]
    vg, glu, gf, gate_s, vg_s, gout, both, whole, weights, in_sem = refs[20:]
    half = (width - 1) // 2
    total, width_in = whole.shape
    depth, channels = weights.shape[1], weights.shape[2] // 2
    strip = pl.program_id(0)
    strips = channels // LANES
    z, y, turn = place[0], place[1], place[2]
    copies = [
        (before.at[:, pl.ds(0, width_in)], whole.at[pl.ds(0, EDGE), :]),
        (inner, whole.at[pl.ds(EDGE, rows), :]),
        (after.at[:, pl.ds(0, width_in)], whole.at[pl.ds(EDGE + rows, EDGE), :]),
        (before.at[:, pl.ds(width_in, channels)], gout.at[pl.ds(0, EDGE), :]),
        (grad_out, gout.at[pl.ds(EDGE, rows), :]),
        (after.at[:, pl.ds(width_in, channels)], gout.at[pl.ds(EDGE + rows, EDGE), :]),
    ]
    for kind in range(2):
        for far in range(RING):
            for near in range(RING):
                if far < RING - 1:
                    source = pieces[5 * kind + far].at[near]
                else:
                    source = pieces[5 * kind + far + near // 2].at[near % 2]
                a, b = (near, far) if kind else (far, near)
                row = lax.rem(z + OFFSETS[a] + RING, RING) * RING
                row = row + lax.rem(y + OFFSETS[b] + RING, RING)
                copies.append((source, weights.at[row, :, pl.ds(kind * channels, channels)]))
    copies = [
        pltpu.make_async_copy(source, target, in_sem.at[n])
        for n, (source, target) in enumerate(copies)
    ]
    @pl.when(strip == 0)
    def _():
        for copy in copies:
            copy.start()
        for copy in copies:
            copy.wait()

    @pl.when(strip < strips)
    def _():
        def columns(kind):
            start = pl.multiple_of(kind * channels + strip * LANES, LANES)
            return weights[:, :, pl.ds(start, LANES)].reshape(RING * RING * depth, LANES)

        vg[...] = jnp.dot(
            whole[...], jnp.concatenate([columns(0), columns(1)], axis=1), preferred_element_type=F32
        )

        def gates(i, _):
            at = pl.ds(pl.multiple_of(i * STRIP, STRIP), STRIP)
            p = jax.nn.sigmoid(vg[at, LANES:])
            vp = vg[at, :LANES] * p
            glu[at, :] = vp.astype(BF16).astype(F32)
            gate_s[at, :] = p
            vg_s[at, :] = vp * (1.0 - p)
            return 0

        lax.fori_loop(0, total // STRIP, gates, 0, unroll=2)
        tap = [jnp.broadcast_to(taps[k : k + 1, :], (8, LANES)) for k in range(width)]

        def conv(source, start, sign):
            parts = [jnp.zeros((8, LANES), F32) for _ in range(STRIP // 8)]
            for k in range(width):
                x = source[pl.ds(start + sign * (k - half), STRIP), :]
                for j in range(STRIP // 8):
                    parts[j] = parts[j] + tap[k] * x[8 * j : 8 * j + 8]
            return jnp.concatenate(parts, axis=0)

        gf[0:EDGE, :] = jnp.zeros((EDGE, LANES), F32)
        gf[total - EDGE : total, :] = jnp.zeros((EDGE, LANES), F32)

        def forward(i, _):
            start = pl.multiple_of(i * STRIP, 16) + EDGE // 2
            at = pl.ds(start, STRIP)
            f = conv(glu, start, 1)
            s = jax.nn.sigmoid(f)
            fs = f * s
            vg[at, :LANES] = fs
            g = gout[at, pl.ds(pl.multiple_of(strip * LANES, LANES), LANES)].astype(F32) * (s + fs * (1.0 - s))
            gf[at, :] = g.astype(BF16).astype(F32)
            return 0

        lax.fori_loop(0, (rows + EDGE) // STRIP, forward, 0, unroll=3)
        act[...] = vg[EDGE : EDGE + rows, :LANES].astype(BF16)

        def backward(i, _):
            start = pl.multiple_of(i * STRIP, STRIP) + EDGE
            at = pl.ds(start, STRIP)
            d = conv(gf, start, -1)
            vg[at, :LANES] = d * gate_s[at, :]
            vg[at, LANES:] = d * vg_s[at, :]
            return 0

        lax.fori_loop(0, rows // STRIP, backward, 0, unroll=2)
        for kind in range(2):
            grad = vg[EDGE : EDGE + rows, kind * LANES : (kind + 1) * LANES]
            start = pl.multiple_of(kind * channels + strip * LANES, LANES)
            both[:, pl.ds(start, LANES)] = grad.astype(BF16)
            turned_both[kind, pl.ds(pl.multiple_of(strip * LANES, LANES), LANES), :] = grad.T.astype(
                BF16
            )

        def tap_sums(i, total_sums):
            start = pl.multiple_of(i * STRIP, STRIP) + EDGE
            q = gf[pl.ds(start, STRIP), :]
            out = []
            for k in range(width):
                x = glu[pl.ds(start + k - half, STRIP), :] * q
                t = total_sums[k]
                for j in range(STRIP // 8):
                    t = t + x[8 * j : 8 * j + 8]
                out.append(t)
            return tuple(out)

        start_sums = tuple(jnp.zeros((8, LANES), F32) for _ in range(width))
        sums = lax.fori_loop(0, rows // STRIP, tap_sums, start_sums)
        for k in range(width):
            gtap[k : k + 1, :] = jnp.sum(sums[k], axis=0, keepdims=True)
        gtap[width:, :] = jnp.zeros((gtap.shape[0] - width, LANES), F32)

    @pl.when((strip >= strips) & (strip < strips + RING * CORES))
    def _():
        block = weights[pl.ds((strip - strips) * CORES, CORES)].reshape(-1, 2 * channels)
        frames_out[...] = lax.dot_general(
            both[...], block, (((1,), (1,)), ((), ())), preferred_element_type=F32
        ).astype(BF16)

    for kind in range(2):

        @pl.when(strip == strips + RING * CORES + kind)
        def _():
            for q in range(RING):
                far = lax.rem(y + RING - turn, RING) if kind else lax.rem(z + RING - turn, RING)
                near = (z if kind else y) + 2 * RING - (q + 1) * turn
                near = lax.rem(near, RING)
                row = near * RING + far if kind else far * RING + near
                part = whole[EDGE : EDGE + rows, pl.ds(pl.multiple_of(row * depth, LANES), depth)]
                first_out[0, q] = jnp.dot(
                    turned_both[kind], part, preferred_element_type=F32
                ).astype(BF16)


def middle(place, pieces, parts, taps):
    rows, inner = parts[1].shape
    total = rows + 2 * EDGE
    depth, channels = pieces[0].shape[1:]
    width = taps.shape[0]
    tall = -(-width // 8) * 8
    taps = jnp.pad(taps.astype(F32), ((0, tall - width), (0, 0)))

    def strips(n):
        return pl.BlockSpec((n, LANES), lambda j, place: (0, jnp.minimum(j, count - 1)))

    def far():
        return pl.BlockSpec(memory_space=pltpu.HBM)

    count = channels // LANES
    part = inner // (RING * CORES)
    begin, end = count, count + RING * CORES

    def frames_block(j, place):
        return (0, jnp.clip(j - begin, 0, RING * CORES - 1))

    def first_block(j, place):
        return (jnp.maximum(j - end, 0), 0, 0, 0)

    shape = jax.ShapeDtypeStruct
    return pl.pallas_call(
        functools.partial(middle_body, width, rows),
        grid_spec=pltpu.PrefetchScalarGridSpec(
            num_scalar_prefetch=1,
            grid=(end + 2,),
            in_specs=[far() for _ in range(len(pieces) + len(parts))] + [strips(tall)],
            out_specs=[
                strips(rows),
                pl.BlockSpec((2, channels, rows), lambda j, place: (0, 0, 0)),
                pl.BlockSpec((rows, part), frames_block),
                pl.BlockSpec((1, RING, channels, depth), first_block),
                strips(tall),
            ],
            scratch_shapes=[pltpu.VMEM((total, 2 * LANES), F32)]
            + [pltpu.VMEM((total, LANES), F32)] * 4
            + [
                pltpu.VMEM((total, channels), BF16),
                pltpu.VMEM((rows, 2 * channels), BF16),
                pltpu.VMEM((total, inner), BF16),
                pltpu.VMEM((RING * RING, depth, 2 * channels), BF16),
                pltpu.SemaphoreType.DMA((2 * RING * RING + 6,)),
            ],
        ),
        out_shape=[
            shape((rows, channels), BF16),
            shape((2, channels, rows), BF16),
            shape((rows, inner), BF16),
            shape((2, RING, channels, depth), BF16),
            shape((tall, channels), F32),
        ],
        compiler_params=pltpu.CompilerParams(vmem_limit_bytes=60 * MIB),
        cost_estimate=pl.CostEstimate(
            flops=40 * 10**9, bytes_accessed=40 * MIB, transcendentals=0
        ),
    )(place, *pieces, *parts, taps)


def weight_body(order, grad, a, b, c, d, out):
    for q, part in enumerate((a, b, c, d)):
        out[0, q] = jnp.dot(grad[0], part[...], preferred_element_type=F32).astype(BF16)


def weight_parts(order, turned_both, whole, depth):
    kinds, channels, rows = turned_both.shape
    count = order.shape[0]

    def block(q):
        return pl.BlockSpec((rows, depth), lambda i, order: (0, order[i, q + 1]))

    return pl.pallas_call(
        weight_body,
        grid_spec=pltpu.PrefetchScalarGridSpec(
            num_scalar_prefetch=1,
            grid=(count,),
            in_specs=[pl.BlockSpec((1, channels, rows), lambda i, order: (order[i, 0], 0, 0))]
            + [block(q) for q in range(RING)],
            out_specs=pl.BlockSpec((1, RING, channels, depth), lambda i, order: (i, 0, 0, 0)),
        ),
        out_shape=jax.ShapeDtypeStruct((count, RING, channels, depth), BF16),
        compiler_params=pltpu.CompilerParams(vmem_limit_bytes=60 * MIB),
        cost_estimate=pl.CostEstimate(
            flops=count * RING * 2 * channels * depth * rows,
            bytes_accessed=count * 4 * MIB,
            transcendentals=0,
        ),
    )(order, turned_both, *[whole] * RING)


def plus(a, *others):
    total = a.astype(F32)
    for other in others:
        total = total + other.astype(F32)
    return total.astype(BF16)


def spread(block, up, down):
    cut = block.shape[0] // 2
    below, above = send(block, up), send(block, down)
    return [block, below, above, send(below[:cut], up), send(above[cut:], down)]


def per_device(frames, w_value, w_gate, taps, grad_out):
    width = taps.shape[0]
    row, col = lax.axis_index("row"), lax.axis_index("col")
    z, y = row // RING, row % RING
    depth = w_value.shape[0]
    turn = way(col % CORES)

    whole = lax.all_gather(frames, "col", axis=1, tiled=True)
    value, gate = spread(w_value, UP_Y, DOWN_Y), spread(w_gate, UP_Z, DOWN_Z)
    near = together(*value, *gate)
    value, gate = near[:5], near[5:]
    shape = (RING,) + w_value.shape
    value = jnp.concatenate(value).reshape(shape)
    gate = jnp.concatenate(gate).reshape(shape)
    pieces = spread(value, UP_Z, DOWN_Z) + spread(gate, UP_Y, DOWN_Y)
    before, after = halo(whole, grad_out)
    place = jnp.stack([z, y, turn]).astype(jnp.int32)
    activated, turned_both, part, first, tap_sum = middle(
        place, pieces, (before, whole, after, grad_out), taps
    )

    def behind(at, step):
        return (at - step * turn) % RING

    def of_weights(step):
        sides = [1, 2, 3, 4]
        value = [0] + [behind(z, step) * RING + behind(y, q) for q in sides]
        gate = [1] + [behind(z, q) * RING + behind(y, step) for q in sides]
        return [value, gate]

    def table(rows):
        return jnp.array(rows, jnp.int32)

    grad_frames = lax.psum_scatter(part, "col", scatter_dimension=1, tiled=True)

    def folded(stride):
        pairs = [(i, i ^ stride) for i in range(RING * RING)]
        return tap_sum + lax.ppermute(tap_sum, "row", pairs)

    tap_sum = folded(1)
    order = of_weights(2) + of_weights(3) + of_weights(4)
    later = weight_parts(table(order), turned_both, whole, depth)
    later, tap_sum = together(later, tap_sum)

    def shares(step, group):
        cut = slice(2 * group, 2 * group + 2)
        if step == 1:
            return first[0, cut], first[1, cut]
        return later[(step - 2) * 2, cut], later[(step - 2) * 2 + 1, cut]

    def onward(held):
        return send(held[0], ALONG_Z), send(held[1], ALONG_Y)

    moving = [onward(shares(1, 0)), onward(shares(1, 1))]
    last = None
    for step in range(2, RING + 1):
        for group in range(2):
            got = moving[group]
            if last is not None:
                got = together(*got, *last)[:2]
            last = tuple(plus(a, b) for a, b in zip(shares(step, group), got))
            moving[group] = onward(last) if step < RING else last
        if step < RING:
            *last, tap_sum = together(*last, tap_sum)
            tap_sum = folded(2 ** (step - 1))
            tap_sum, *moving[0] = together(tap_sum, *moving[0])
    tap_sum, *moving[0] = together(tap_sum, *moving[0])
    tap_sum = folded(8)
    near = [
        (send(moving[0][kind][0], along), send(moving[0][kind][1], two))
        for kind, along, two in ((0, BACK_Y, TWO_Y), (1, BACK_Z, TWO_Z))
    ]
    grads = []
    for kind, pairs in ((0, ALONG_Y), (1, ALONG_Z)):
        got = send(moving[1][kind][0], pairs)
        grads.append(plus(moving[1][kind][1], *near[kind], got).T)
    return (activated, grad_frames, *grads, tap_sum[:width])


def solution(mesh):
    in_specs = (P("row", "col"), P("row", "col"), P("row", "col"), P(None, "col"), P("row", "col"))
    out_specs = (P("row", "col"), P("row", "col"), P("row", "col"), P("row", "col"), P(None, "col"))
    return jax.shard_map(
        per_device, mesh=mesh, in_specs=in_specs, out_specs=out_specs, check_vma=False
    )
```

```python
import functools

import jax
import jax.numpy as jnp
from jax import lax
from jax.experimental import pallas as pl
from jax.experimental.pallas import tpu as pltpu
from jax.sharding import PartitionSpec as P

F32 = jnp.float32
BF16 = jnp.bfloat16
BOTH = ("row", "col")
RING = 4
CORES = 2
EDGE = 32
LANES = 128
STRIP = 32
MIB = 2**20


def turning(step):
    pairs = []
    for source in range(RING * RING * RING * CORES):
        rest, core = source // CORES, source % CORES
        at = [rest // RING**2, rest // RING % RING, rest % RING]
        at, core = step(at, core)
        z, y, x = (place % RING for place in at)
        pairs.append((source, ((z * RING + y) * RING + x) * CORES + core))
    return pairs


def way(core):
    return 1 - 2 * core


ALONG_Y = turning(lambda at, core: ((at[0], at[1] + way(core), at[2]), core))
ALONG_Z = turning(lambda at, core: ((at[0] + way(core), at[1], at[2]), core))
BACK_Y = turning(lambda at, core: ((at[0], at[1] - way(core), at[2]), core))
BACK_Z = turning(lambda at, core: ((at[0] - way(core), at[1], at[2]), core))
TWO_Y = turning(lambda at, core: ((at[0], at[1] + 2, at[2]), core))
TWO_Z = turning(lambda at, core: ((at[0] + 2, at[1], at[2]), core))
UP_Y = turning(lambda at, core: ((at[0], at[1] + 1, at[2]), core))
UP_Z = turning(lambda at, core: ((at[0] + 1, at[1], at[2]), core))
DOWN_Y = turning(lambda at, core: ((at[0], at[1] - 1, at[2]), core))
DOWN_Z = turning(lambda at, core: ((at[0] - 1, at[1], at[2]), core))
OFFSETS = (0, -1, 1, 2)


def send(array, pairs):
    return lax.ppermute(array, BOTH, pairs)


def halo(*arrays):
    count, length = lax.axis_size("row"), arrays[0].shape[0]
    up = [(i, i + 1) for i in range(count - 1)]
    down = [(j, i) for i, j in up]
    last = jnp.concatenate([array[length - EDGE :] for array in arrays], axis=1)
    first = jnp.concatenate([array[:EDGE] for array in arrays], axis=1)
    return lax.ppermute(last, "row", up), lax.ppermute(first, "row", down)


def together(*values):
    return lax.optimization_barrier(values)


def middle_body(width, rows, place, *refs):
    pieces, (before, inner, after, grad_out), taps = refs[:10], refs[10:14], refs[14]
    act, turned_both, frames_out, first_out, gtap = refs[15:20]
    vg, glu, gf, gate_s, vg_s, gout, both, whole, weights, in_sem = refs[20:]
    half = (width - 1) // 2
    total, width_in = whole.shape
    depth, channels = weights.shape[1], weights.shape[2] // 2
    strip = pl.program_id(0)
    strips = channels // LANES
    z, y, turn = place[0], place[1], place[2]
    copies = [
        (before.at[:, pl.ds(0, width_in)], whole.at[pl.ds(0, EDGE), :]),
        (inner, whole.at[pl.ds(EDGE, rows), :]),
        (after.at[:, pl.ds(0, width_in)], whole.at[pl.ds(EDGE + rows, EDGE), :]),
        (before.at[:, pl.ds(width_in, channels)], gout.at[pl.ds(0, EDGE), :]),
        (grad_out, gout.at[pl.ds(EDGE, rows), :]),
        (after.at[:, pl.ds(width_in, channels)], gout.at[pl.ds(EDGE + rows, EDGE), :]),
    ]
    strip_copies = [[] for _ in range(strips)]
    for kind in range(2):
        for far in range(RING):
            for near in range(RING):
                if far < RING - 1:
                    source = pieces[5 * kind + far].at[near]
                else:
                    source = pieces[5 * kind + far + near // 2].at[near % 2]
                a, b = (near, far) if kind else (far, near)
                row = lax.rem(z + OFFSETS[a] + RING, RING) * RING
                row = row + lax.rem(y + OFFSETS[b] + RING, RING)
                for part in range(strips):
                    start = kind * channels + part * LANES
                    target = weights.at[row, :, pl.ds(start, LANES)]
                    strip_copies[part].append((source.at[:, pl.ds(part * LANES, LANES)], target))
    strip_copies[0] = copies + strip_copies[0]
    count = 0
    for part in range(strips):
        for n, (source, target) in enumerate(strip_copies[part]):
            strip_copies[part][n] = pltpu.make_async_copy(source, target, in_sem.at[count])
            count += 1

    @pl.when(strip == 0)
    def _():
        for copies in strip_copies:
            for copy in copies:
                copy.start()

    for part in range(strips):

        @pl.when(strip == part)
        def _():
            for copy in strip_copies[part]:
                copy.wait()

    @pl.when(strip < strips)
    def _():
        def columns(kind):
            start = pl.multiple_of(kind * channels + strip * LANES, LANES)
            return weights[:, :, pl.ds(start, LANES)].reshape(RING * RING * depth, LANES)

        vg[...] = jnp.dot(
            whole[...], jnp.concatenate([columns(0), columns(1)], axis=1), preferred_element_type=F32
        )

        def gates(i, _):
            at = pl.ds(pl.multiple_of(i * STRIP, STRIP), STRIP)
            p = jax.nn.sigmoid(vg[at, LANES:])
            vp = vg[at, :LANES] * p
            glu[at, :] = vp.astype(BF16).astype(F32)
            gate_s[at, :] = p
            vg_s[at, :] = vp * (1.0 - p)
            return 0

        lax.fori_loop(0, total // STRIP, gates, 0, unroll=2)
        tap = [jnp.broadcast_to(taps[k : k + 1, :], (8, LANES)) for k in range(width)]

        def conv(source, start, sign):
            parts = [jnp.zeros((8, LANES), F32) for _ in range(STRIP // 8)]
            for k in range(width):
                x = source[pl.ds(start + sign * (k - half), STRIP), :]
                for j in range(STRIP // 8):
                    parts[j] = parts[j] + tap[k] * x[8 * j : 8 * j + 8]
            return jnp.concatenate(parts, axis=0)

        gf[0:EDGE, :] = jnp.zeros((EDGE, LANES), F32)
        gf[total - EDGE : total, :] = jnp.zeros((EDGE, LANES), F32)

        def forward(i, _):
            start = pl.multiple_of(i * STRIP, 16) + EDGE // 2
            at = pl.ds(start, STRIP)
            f = conv(glu, start, 1)
            s = jax.nn.sigmoid(f)
            fs = f * s
            vg[at, :LANES] = fs
            g = gout[at, pl.ds(pl.multiple_of(strip * LANES, LANES), LANES)].astype(F32) * (s + fs * (1.0 - s))
            gf[at, :] = g.astype(BF16).astype(F32)
            return 0

        lax.fori_loop(0, (rows + EDGE) // STRIP, forward, 0, unroll=3)
        act[...] = vg[EDGE : EDGE + rows, :LANES].astype(BF16)

        def backward(i, _):
            start = pl.multiple_of(i * STRIP, STRIP) + EDGE
            at = pl.ds(start, STRIP)
            d = conv(gf, start, -1)
            vg[at, :LANES] = d * gate_s[at, :]
            vg[at, LANES:] = d * vg_s[at, :]
            return 0

        lax.fori_loop(0, rows // STRIP, backward, 0, unroll=2)
        for kind in range(2):
            grad = vg[EDGE : EDGE + rows, kind * LANES : (kind + 1) * LANES]
            start = pl.multiple_of(kind * channels + strip * LANES, LANES)
            both[:, pl.ds(start, LANES)] = grad.astype(BF16)
            turned_both[kind, pl.ds(pl.multiple_of(strip * LANES, LANES), LANES), :] = grad.T.astype(
                BF16
            )

        def tap_sums(i, total_sums):
            start = pl.multiple_of(i * STRIP, STRIP) + EDGE
            q = gf[pl.ds(start, STRIP), :]
            out = []
            for k in range(width):
                x = glu[pl.ds(start + k - half, STRIP), :] * q
                t = total_sums[k]
                for j in range(STRIP // 8):
                    t = t + x[8 * j : 8 * j + 8]
                out.append(t)
            return tuple(out)

        start_sums = tuple(jnp.zeros((8, LANES), F32) for _ in range(width))
        sums = lax.fori_loop(0, rows // STRIP, tap_sums, start_sums)
        for k in range(width):
            gtap[k : k + 1, :] = jnp.sum(sums[k], axis=0, keepdims=True)
        gtap[width:, :] = jnp.zeros((gtap.shape[0] - width, LANES), F32)

    @pl.when((strip >= strips) & (strip < strips + RING * CORES))
    def _():
        block = weights[pl.ds((strip - strips) * CORES, CORES)].reshape(-1, 2 * channels)
        frames_out[...] = lax.dot_general(
            both[...], block, (((1,), (1,)), ((), ())), preferred_element_type=F32
        ).astype(BF16)

    for kind in range(2):

        @pl.when(strip == strips + RING * CORES + kind)
        def _():
            for q in range(RING):
                far = lax.rem(y + RING - turn, RING) if kind else lax.rem(z + RING - turn, RING)
                near = (z if kind else y) + 2 * RING - (q + 1) * turn
                near = lax.rem(near, RING)
                row = near * RING + far if kind else far * RING + near
                part = whole[EDGE : EDGE + rows, pl.ds(pl.multiple_of(row * depth, LANES), depth)]
                first_out[0, q] = jnp.dot(
                    turned_both[kind], part, preferred_element_type=F32
                ).astype(BF16)


def middle(place, pieces, parts, taps):
    rows, inner = parts[1].shape
    total = rows + 2 * EDGE
    depth, channels = pieces[0].shape[1:]
    width = taps.shape[0]
    tall = -(-width // 8) * 8
    taps = jnp.pad(taps.astype(F32), ((0, tall - width), (0, 0)))

    def strips(n):
        return pl.BlockSpec((n, LANES), lambda j, place: (0, jnp.minimum(j, count - 1)))

    def far():
        return pl.BlockSpec(memory_space=pltpu.HBM)

    count = channels // LANES
    part = inner // (RING * CORES)
    begin, end = count, count + RING * CORES

    def frames_block(j, place):
        return (0, jnp.clip(j - begin, 0, RING * CORES - 1))

    def first_block(j, place):
        return (jnp.maximum(j - end, 0), 0, 0, 0)

    shape = jax.ShapeDtypeStruct
    return pl.pallas_call(
        functools.partial(middle_body, width, rows),
        grid_spec=pltpu.PrefetchScalarGridSpec(
            num_scalar_prefetch=1,
            grid=(end + 2,),
            in_specs=[far() for _ in range(len(pieces) + len(parts))] + [strips(tall)],
            out_specs=[
                strips(rows),
                pl.BlockSpec((2, channels, rows), lambda j, place: (0, 0, 0)),
                pl.BlockSpec((rows, part), frames_block),
                pl.BlockSpec((1, RING, channels, depth), first_block),
                strips(tall),
            ],
            scratch_shapes=[pltpu.VMEM((total, 2 * LANES), F32)]
            + [pltpu.VMEM((total, LANES), F32)] * 4
            + [
                pltpu.VMEM((total, channels), BF16),
                pltpu.VMEM((rows, 2 * channels), BF16),
                pltpu.VMEM((total, inner), BF16),
                pltpu.VMEM((RING * RING, depth, 2 * channels), BF16),
                pltpu.SemaphoreType.DMA((2 * RING * RING * count + 6,)),
            ],
        ),
        out_shape=[
            shape((rows, channels), BF16),
            shape((2, channels, rows), BF16),
            shape((rows, inner), BF16),
            shape((2, RING, channels, depth), BF16),
            shape((tall, channels), F32),
        ],
        compiler_params=pltpu.CompilerParams(vmem_limit_bytes=60 * MIB),
        cost_estimate=pl.CostEstimate(
            flops=40 * 10**9, bytes_accessed=40 * MIB, transcendentals=0
        ),
    )(place, *pieces, *parts, taps)


def weight_body(order, grad, a, b, c, d, out):
    for q, part in enumerate((a, b, c, d)):
        out[0, q] = jnp.dot(grad[0], part[...], preferred_element_type=F32).astype(BF16)


def weight_parts(order, turned_both, whole, depth):
    kinds, channels, rows = turned_both.shape
    count = order.shape[0]

    def block(q):
        return pl.BlockSpec((rows, depth), lambda i, order: (0, order[i, q + 1]))

    return pl.pallas_call(
        weight_body,
        grid_spec=pltpu.PrefetchScalarGridSpec(
            num_scalar_prefetch=1,
            grid=(count,),
            in_specs=[pl.BlockSpec((1, channels, rows), lambda i, order: (order[i, 0], 0, 0))]
            + [block(q) for q in range(RING)],
            out_specs=pl.BlockSpec((1, RING, channels, depth), lambda i, order: (i, 0, 0, 0)),
        ),
        out_shape=jax.ShapeDtypeStruct((count, RING, channels, depth), BF16),
        compiler_params=pltpu.CompilerParams(vmem_limit_bytes=60 * MIB),
        cost_estimate=pl.CostEstimate(
            flops=count * RING * 2 * channels * depth * rows,
            bytes_accessed=count * 4 * MIB,
            transcendentals=0,
        ),
    )(order, turned_both, *[whole] * RING)


def plus(a, *others):
    total = a.astype(F32)
    for other in others:
        total = total + other.astype(F32)
    return total.astype(BF16)


def spread(block, up, down):
    cut = block.shape[0] // 2
    below, above = send(block, up), send(block, down)
    return [block, below, above, send(below[:cut], up), send(above[cut:], down)]


def per_device(frames, w_value, w_gate, taps, grad_out):
    width = taps.shape[0]
    row, col = lax.axis_index("row"), lax.axis_index("col")
    z, y = row // RING, row % RING
    depth = w_value.shape[0]
    turn = way(col % CORES)

    whole = lax.all_gather(frames, "col", axis=1, tiled=True)
    value, gate = spread(w_value, UP_Y, DOWN_Y), spread(w_gate, UP_Z, DOWN_Z)
    near = together(*value, *gate)
    value, gate = near[:5], near[5:]
    shape = (RING,) + w_value.shape
    value = jnp.concatenate(value).reshape(shape)
    gate = jnp.concatenate(gate).reshape(shape)
    pieces = spread(value, UP_Z, DOWN_Z) + spread(gate, UP_Y, DOWN_Y)
    before, after = halo(whole, grad_out)
    place = jnp.stack([z, y, turn]).astype(jnp.int32)
    activated, turned_both, part, first, tap_sum = middle(
        place, pieces, (before, whole, after, grad_out), taps
    )

    def behind(at, step):
        return (at - step * turn) % RING

    def of_weights(step):
        sides = [1, 2, 3, 4]
        value = [0] + [behind(z, step) * RING + behind(y, q) for q in sides]
        gate = [1] + [behind(z, q) * RING + behind(y, step) for q in sides]
        return [value, gate]

    def table(rows):
        return jnp.array(rows, jnp.int32)

    grad_frames = lax.psum_scatter(part, "col", scatter_dimension=1, tiled=True)

    def folded(stride):
        pairs = [(i, i ^ stride) for i in range(RING * RING)]
        return tap_sum + lax.ppermute(tap_sum, "row", pairs)

    tap_sum = folded(1)
    order = of_weights(2) + of_weights(3) + of_weights(4)
    later = weight_parts(table(order), turned_both, whole, depth)
    later, tap_sum = together(later, tap_sum)

    def shares(step, group):
        cut = slice(2 * group, 2 * group + 2)
        if step == 1:
            return first[0, cut], first[1, cut]
        return later[(step - 2) * 2, cut], later[(step - 2) * 2 + 1, cut]

    def onward(held):
        return send(held[0], ALONG_Z), send(held[1], ALONG_Y)

    moving = [onward(shares(1, 0)), onward(shares(1, 1))]
    last = None
    for step in range(2, RING + 1):
        for group in range(2):
            got = moving[group]
            if last is not None:
                got = together(*got, *last)[:2]
            last = tuple(plus(a, b) for a, b in zip(shares(step, group), got))
            moving[group] = onward(last) if step < RING else last
        if step < RING:
            *last, tap_sum = together(*last, tap_sum)
            tap_sum = folded(2 ** (step - 1))
            tap_sum, *moving[0] = together(tap_sum, *moving[0])
    tap_sum, *moving[0] = together(tap_sum, *moving[0])
    tap_sum = folded(8)
    near = [
        (send(moving[0][kind][0], along), send(moving[0][kind][1], two))
        for kind, along, two in ((0, BACK_Y, TWO_Y), (1, BACK_Z, TWO_Z))
    ]
    grads = []
    for kind, pairs in ((0, ALONG_Y), (1, ALONG_Z)):
        got = send(moving[1][kind][0], pairs)
        grads.append(plus(moving[1][kind][1], *near[kind], got).T)
    return (activated, grad_frames, *grads, tap_sum[:width])


def solution(mesh):
    in_specs = (P("row", "col"), P("row", "col"), P("row", "col"), P(None, "col"), P("row", "col"))
    out_specs = (P("row", "col"), P("row", "col"), P("row", "col"), P("row", "col"), P(None, "col"))
    return jax.shard_map(
        per_device, mesh=mesh, in_specs=in_specs, out_specs=out_specs, check_vma=False
    )
```
